256 devices in a mesh: blk: 32 (over z_lo, y, core), uly: 8 (over z_hi, x).
Axes of the slice: x: 4, y: 4, z: 8 (z_hi: 2, z_lo: 4; z = z_hi * 4 + z_lo), core: 2. Of those that a mesh axis runs over, the one named last changes fastest.
Arguments:
- tokens: bfloat16 [24576, 3072], P(('blk', 'uly')), may hold values from -32 to 32
- qkv_weight: bfloat16 [3072, 3, 3072], P(None, None, 'uly'), may hold values from -1 to 1
- out_weight: bfloat16 [3072, 3072], P('uly'), may hold values from -0.109375 to 0.109375
Outputs:
- mixed: bfloat16 [24576, 3072], P(('blk', 'uly'))
The draws below stay inside these ranges and needn't reach their ends.
All inputs are finite; a program needn't handle non-finite values.
Results may differ from the reference program's by a relative error of at most 0.011.
Values may be sent and summed in bfloat16 or wider, within the bound.
No kernel may reach another device: no remote copies, remote signals or barrier semaphores. Data moves between devices by JAX's collectives and lax.ppermute only.
A program may use at most 128 MiB of HBM per device.

```python
import math
import jax
import jax.numpy as jnp
from jax import lax

D = 3072
HEADS = 24
HEAD_DIM = 128
WINDOW = 4
GROUP = 768
TOKENS = 24576
N_BLK = 32


def draw_tokens(key, part):
    key = jax.random.fold_in(key, 11)
    base_key = jax.random.fold_in(key, 0)
    base = jax.random.normal(base_key, (TOKENS, D), jnp.float32)
    values = 1.6 * base
    return jnp.clip(values, -32.0, 32.0).astype(jnp.bfloat16)


def draw_qkv_weight(key, part):
    key = jax.random.fold_in(key, 23)
    width = HEADS * HEAD_DIM
    values = jax.random.normal(key, (D, 3, width), jnp.float32) / math.sqrt(D)
    return jnp.clip(values, -1.0, 1.0).astype(jnp.bfloat16)


def shard_levels(key, extent, cuts, smallest, top_value):
    def one(dim, blocks):
        draws = jax.random.uniform(jax.random.fold_in(jax.random.fold_in(key, 6), dim), (blocks,), jnp.float32, smallest / len(cuts), top_value / len(cuts))
        return jnp.repeat(jnp.exp(draws), extent[dim] // blocks).reshape((-1,) + (1,) * (len(extent) - dim - 1))

    loudness = one(*cuts[0])
    for cut in cuts[1:]:
        loudness = loudness * one(*cut)
    return loudness


def gaussian(key, dims, scale, limit, cuts=(), held_as=jnp.bfloat16):
    entries = jax.random.normal(key, dims, jnp.float32) * scale
    if len(cuts) > 0:
        entries = shard_levels(key, dims, cuts, -0.22, 0.18) * entries
    return jnp.clip(entries, min=-limit, max=limit).astype(held_as)


def setup_inputs(seed: int = 0) -> dict:
    keys = jax.random.split(jax.random.key(seed), 4)
    tokens = draw_tokens(jax.random.fold_in(keys[3], 71), 0)
    qkv_weight = draw_qkv_weight(jax.random.fold_in(keys[3], 71), 0)
    out_weight = gaussian(keys[2], (HEADS * HEAD_DIM, D), (HEADS * HEAD_DIM) ** -0.5, 0.109375, ((0, 8),))
    return dict(tokens=tokens, qkv_weight=qkv_weight, out_weight=out_weight)


def reference(tokens, qkv_weight, out_weight):
    width = HEADS * HEAD_DIM
    flat_weight = qkv_weight.reshape(D, 3 * width)
    projected = jnp.dot(tokens, flat_weight, preferred_element_type=jnp.float32).astype(jnp.bfloat16)
    projected = projected.reshape(N_BLK, GROUP, 3, HEADS, HEAD_DIM)
    queries = projected[:, :, 0]
    keys_all = projected[:, :, 1]
    values_all = projected[:, :, 2]
    scale = 1.0 / math.sqrt(HEAD_DIM)

    def one_group(index):
        query_block = lax.dynamic_index_in_dim(queries, index, 0, keepdims=False).astype(jnp.float32)
        maxima = []
        totals = []
        outputs = []
        for offset in range(WINDOW):
            source = ((index + offset) % N_BLK).astype(jnp.int32)
            key_block = lax.dynamic_index_in_dim(keys_all, source, 0, keepdims=False).astype(jnp.float32)
            value_block = lax.dynamic_index_in_dim(values_all, source, 0, keepdims=False).astype(jnp.float32)
            scores = jnp.einsum('qhd,khd->hqk', query_block, key_block) * scale
            maximum = lax.optimization_barrier(jnp.max(scores, axis=2))
            weights = jnp.exp(scores - maximum[:, :, None])
            total = lax.optimization_barrier(jnp.sum(weights, axis=2))
            rounded = lax.optimization_barrier(weights.astype(jnp.bfloat16)).astype(jnp.float32)
            partial_out = jnp.einsum('hqk,khd->hqd', rounded, value_block)
            maxima.append(maximum)
            totals.append(total)
            outputs.append(partial_out)
        stacked_max = jnp.stack(maxima, axis=0)
        top = lax.optimization_barrier(jnp.max(stacked_max, axis=0))
        factors = jnp.exp(stacked_max - top[None])
        numerator = lax.optimization_barrier(jnp.sum(factors[:, :, :, None] * jnp.stack(outputs, axis=0), axis=0))
        denominator = lax.optimization_barrier(jnp.sum(factors * jnp.stack(totals, axis=0), axis=0))
        attended = numerator / denominator[:, :, None]
        return attended.transpose(1, 0, 2).reshape(GROUP, width).astype(jnp.bfloat16)
    attended_all = lax.map(one_group, jnp.arange(N_BLK, dtype=jnp.int32)).reshape(TOKENS, width)
    return jnp.dot(attended_all, out_weight, preferred_element_type=jnp.float32).astype(jnp.bfloat16)
```

```python
import functools
import math

import jax
import jax.numpy as jnp
from jax import lax
from jax.experimental import pallas as pl
from jax.experimental.pallas import tpu as pltpu
from jax.sharding import PartitionSpec as P

HEAD_DIM = 128
Z_LO, Y, CORE, Z_HI, X = 4, 4, 2, 2, 4
BOTH = ("blk", "uly")
EXP2_SCALE = math.log2(math.e) / math.sqrt(HEAD_DIM)
VMEM_LIMIT = 48 * 1024 * 1024


def route(move):
    pairs = []
    for place in range(Z_LO * Y * CORE * Z_HI * X):
        blk, uly = divmod(place, Z_HI * X)
        chip, core = divmod(blk, CORE)
        z_hi, x = divmod(uly, X)
        target = move(chip, core, z_hi, x)
        if target is not None:
            chip2, core2, z_hi2, x2 = target
            blk2 = (chip2 % (Z_LO * Y)) * CORE + core2
            pairs.append((place, blk2 * Z_HI * X + (z_hi2 % Z_HI) * X + x2 % X))
    return pairs


def send(block, move):
    return lax.ppermute(block, BOTH, route(move))


def first_way(chip, core, z_hi, x):
    return chip, core, z_hi, x + (1 if core == 0 else -1)


def other_way(chip, core, z_hi, x):
    return chip, core, z_hi, x - (1 if core == 0 else -1)


def across_z(chip, core, z_hi, x):
    return chip, core, z_hi + 1, x


def other_core(chip, core, z_hi, x):
    return chip, 1 - core, z_hi, x


def chip_before(chip, core, z_hi, x):
    return chip - 1, core, z_hi, x


def last_group(chip, core, z_hi, x):
    return (chip, 0, z_hi, x) if core == 1 else (chip - 1, 1, z_hi, x)


def project_kernel(own, first, other, far, weight, queries, pairs, rows):
    part = pl.program_id(0)
    n = own.shape[0]

    @pl.when(part == 0)
    def _():
        for slot, ref in enumerate((own, first, other, far)):
            rows[slot * n : (slot + 1) * n, :] = ref[...]

    result = jnp.dot(rows[...], weight[0], preferred_element_type=jnp.float32).astype(jnp.bfloat16)

    @pl.when(part == 0)
    def _():
        queries[...] = result

    @pl.when(part > 0)
    def _():
        pairs[...] = result


def project(slots, weight):
    n, width = slots[0].shape
    head_width = weight.shape[2]
    m = 4 * n
    return pl.pallas_call(
        project_kernel,
        grid=(3,),
        in_specs=[pl.BlockSpec((n, width), lambda j: (0, 0))] * 4
        + [pl.BlockSpec((1, width, head_width), lambda j: (j, 0, 0))],
        out_specs=[
            pl.BlockSpec((m, head_width), lambda j: (0, 0)),
            pl.BlockSpec((m, head_width), lambda j: (0, jnp.maximum(j - 1, 0))),
        ],
        out_shape=[
            jax.ShapeDtypeStruct((m, head_width), jnp.bfloat16),
            jax.ShapeDtypeStruct((m, 2 * head_width), jnp.bfloat16),
        ],
        scratch_shapes=[pltpu.VMEM((m, width), jnp.bfloat16)],
        compiler_params=pltpu.CompilerParams(vmem_limit_bytes=VMEM_LIMIT),
        cost_estimate=pl.CostEstimate(
            flops=2 * m * width * 3 * head_width, bytes_accessed=2 * 3 * width * head_width, transcendentals=0
        ),
    )(*slots, weight)


def attend_kernel(n_queries, n_pairs, *refs):
    queries = refs[:n_queries]
    pairs = refs[n_queries : n_queries + n_pairs]
    out, q_all, kv_all, sems = refs[n_queries + n_pairs :]
    m, head_width = queries[0].shape
    rows = pairs[0].shape[0]
    copies = [pltpu.make_async_copy(ref, q_all.at[i], sems.at[i]) for i, ref in enumerate(queries)]
    copies += [
        pltpu.make_async_copy(ref, kv_all.at[pl.ds(i * rows, rows), :], sems.at[n_queries + i])
        for i, ref in enumerate(pairs)
    ]
    for copy in copies:
        copy.start()
    for copy in copies:
        copy.wait()
    keys = n_pairs * rows
    step = 768

    @pl.loop(0, n_queries)
    def _(chunk):
        for head in range(head_width // HEAD_DIM):
            columns = slice(head * HEAD_DIM, (head + 1) * HEAD_DIM)
            values = slice(head_width + head * HEAD_DIM, head_width + (head + 1) * HEAD_DIM)
            query = q_all[chunk, :, columns]
            scores = [
                lax.dot_general(
                    query,
                    kv_all[k : k + step, columns],
                    (((1,), (1,)), ((), ())),
                    preferred_element_type=jnp.float32,
                )
                for k in range(0, keys, step)
            ]
            top = functools.reduce(jnp.maximum, [jnp.max(s, axis=1, keepdims=True) for s in scores])
            total = jnp.zeros((m, 1), jnp.float32)
            mixed = jnp.zeros((m, HEAD_DIM), jnp.float32)
            for i, s in enumerate(scores):
                weights = jnp.exp2((s - top) * EXP2_SCALE)
                total = total + jnp.sum(weights, axis=1, keepdims=True)
                mixed = mixed + jnp.dot(
                    weights.astype(jnp.bfloat16),
                    kv_all[i * step : (i + 1) * step, values],
                    preferred_element_type=jnp.float32,
                )
            out[chunk, :, columns] = (mixed / total).astype(jnp.bfloat16)


def attend(queries, pairs):
    m, head_width = queries[0].shape
    rows = pairs[0].shape[0]
    keys = len(pairs) * rows
    pairs_work = len(queries) * m * keys * head_width
    return pl.pallas_call(
        functools.partial(attend_kernel, len(queries), len(pairs)),
        in_specs=[pl.BlockSpec(memory_space=pl.ANY)] * (len(queries) + len(pairs)),
        out_specs=pl.BlockSpec(memory_space=pltpu.VMEM),
        out_shape=jax.ShapeDtypeStruct((len(queries), m, head_width), jnp.bfloat16),
        scratch_shapes=[
            pltpu.VMEM((len(queries), m, head_width), jnp.bfloat16),
            pltpu.VMEM((keys, 2 * head_width), jnp.bfloat16),
            pltpu.SemaphoreType.DMA((len(queries) + len(pairs),)),
        ],
        compiler_params=pltpu.CompilerParams(vmem_limit_bytes=VMEM_LIMIT),
        cost_estimate=pl.CostEstimate(
            flops=4 * pairs_work, bytes_accessed=4 * keys * head_width, transcendentals=pairs_work // HEAD_DIM
        ),
    )(*queries, *pairs)


def on_device(tokens, qkv_weight, out_weight):
    rows = tokens.shape[0]
    half = rows // 2
    own_chunks = [tokens[:half], tokens[half:]]
    far_chunks = [send(chunk, across_z) for chunk in own_chunks]
    weight = jnp.transpose(qkv_weight, (1, 0, 2))

    queries, all_pairs = [], []
    for chunk in own_chunks + far_chunks:
        first = send(chunk, first_way)
        other = send(chunk, other_way)
        far = send(first, first_way)
        chunk_queries, own_pairs = project((chunk, first, other, far), weight)
        queries.append(chunk_queries)
        two_on = send(own_pairs, chip_before)
        swapped = send(two_on, other_core)
        is_second = lax.axis_index("blk") % CORE == 1
        last = send(jnp.where(is_second, own_pairs, two_on), last_group)
        all_pairs += [own_pairs, two_on, swapped, last]

    share = out_weight.shape[0] // (Y * CORE)
    place = lax.axis_index("blk") % (Y * CORE)
    piece = lax.dynamic_slice_in_dim(out_weight, place * share, share, 0)
    piece = send(piece, across_z)
    groups = [[i * Y * CORE + j for j in range(Y * CORE)] for i in range(Z_LO)]
    partner_weight = lax.all_gather(piece, "blk", axis=0, tiled=True, axis_index_groups=groups)

    attended = attend(queries, all_pairs)
    outputs = []
    for part in range(2):
        received = send(attended[2 + part], across_z)
        partial = jnp.dot(attended[part], out_weight, preferred_element_type=jnp.float32) + jnp.dot(
            received, partner_weight, preferred_element_type=jnp.float32
        )
        own, first, other, far = (partial[i * half : (i + 1) * half] for i in range(4))
        from_far = send(far.astype(jnp.bfloat16), other_way)
        from_other = send(other.astype(jnp.bfloat16), first_way)
        from_first = send((first + from_far.astype(jnp.float32)).astype(jnp.bfloat16), other_way)
        outputs.append(
            (own + from_other.astype(jnp.float32) + from_first.astype(jnp.float32)).astype(jnp.bfloat16)
        )
    return jnp.concatenate(outputs, axis=0)


def solution(mesh):
    in_specs = (P(("blk", "uly"), None), P(None, None, "uly"), P("uly", None))
    out_specs = P(("blk", "uly"), None)
    return jax.shard_map(
        on_device, mesh=mesh, in_specs=in_specs, out_specs=out_specs, check_vma=False
    )
```

```python
import functools
import math

import jax
import jax.numpy as jnp
from jax import lax
from jax.experimental import pallas as pl
from jax.experimental.pallas import tpu as pltpu
from jax.sharding import PartitionSpec as P

HEAD_DIM = 128
Z_LO, Y, CORE, Z_HI, X = 4, 4, 2, 2, 4
BOTH = ("blk", "uly")
EXP2_SCALE = math.log2(math.e) / math.sqrt(HEAD_DIM)


def route(move):
    pairs = []
    for place in range(Z_LO * Y * CORE * Z_HI * X):
        blk, uly = divmod(place, Z_HI * X)
        chip, core = divmod(blk, CORE)
        z_hi, x = divmod(uly, X)
        target = move(chip, core, z_hi, x)
        if target is not None:
            chip2, core2, z_hi2, x2 = target
            blk2 = (chip2 % (Z_LO * Y)) * CORE + core2
            pairs.append((place, blk2 * Z_HI * X + (z_hi2 % Z_HI) * X + x2 % X))
    return pairs


def send(block, move):
    return lax.ppermute(block, BOTH, route(move))


def first_way(chip, core, z_hi, x):
    return chip, core, z_hi, x + (1 if core == 0 else -1)


def other_way(chip, core, z_hi, x):
    return chip, core, z_hi, x - (1 if core == 0 else -1)


def across_z(chip, core, z_hi, x):
    return chip, core, z_hi + 1, x


def other_core(chip, core, z_hi, x):
    return chip, 1 - core, z_hi, x


def chip_before(chip, core, z_hi, x):
    return chip - 1, core, z_hi, x


def last_group(chip, core, z_hi, x):
    return (chip, 0, z_hi, x) if core == 1 else (chip - 1, 1, z_hi, x)


def after(block, *earlier):
    return lax.optimization_barrier((block,) + earlier)[0]


VMEM = pl.BlockSpec(memory_space=pltpu.VMEM)
ANY = pl.BlockSpec(memory_space=pl.ANY)


def params(mebibytes):
    return pltpu.CompilerParams(vmem_limit_bytes=mebibytes * 1024 * 1024)


def cost(flops, reads):
    return pl.CostEstimate(flops=flops, bytes_accessed=reads, transcendentals=0)


def copy_all(copies):
    for copy in copies:
        copy.start()
    for copy in copies:
        copy.wait()


def project_kernel(pieces, own, first, other, far, weight, queries, pairs, rows, held, sems):
    n = own.shape[0]
    depth, head_width = weight.shape[1:]
    piece = depth // pieces
    loads = []
    for i, part in enumerate((1, 2, 0)):
        for k in range(pieces):
            source = weight.at[part, pl.ds(k * piece, piece), :]
            at = i * pieces + k
            loads.append(pltpu.make_async_copy(source, held.at[at], sems.at[at]))
    for load in loads:
        load.start()
    for slot, ref in enumerate((own, first, other, far)):
        rows[slot * n : (slot + 1) * n, :] = ref[...]
    for i in range(3):
        total = jnp.zeros((4 * n, head_width), jnp.float32)
        for k in range(pieces):
            at = i * pieces + k
            loads[at].wait()
            total = total + jnp.dot(
                rows[:, k * piece : (k + 1) * piece], held[at], preferred_element_type=jnp.float32
            )
        if i < 2:
            pairs[:, i * head_width : (i + 1) * head_width] = total.astype(jnp.bfloat16)
        else:
            queries[...] = total.astype(jnp.bfloat16)


def project(slots, weight):
    n, width = slots[0].shape
    head_width = weight.shape[2]
    m = 4 * n
    pieces = 2
    return pl.pallas_call(
        functools.partial(project_kernel, pieces),
        in_specs=[VMEM] * 4 + [ANY],
        out_specs=[VMEM] * 2,
        out_shape=[
            jax.ShapeDtypeStruct((m, head_width), jnp.bfloat16),
            jax.ShapeDtypeStruct((m, 2 * head_width), jnp.bfloat16),
        ],
        scratch_shapes=[
            pltpu.VMEM((m, width), jnp.bfloat16),
            pltpu.VMEM((3 * pieces, width // pieces, head_width), jnp.bfloat16),
            pltpu.SemaphoreType.DMA((3 * pieces,)),
        ],
        compiler_params=params(48),
        cost_estimate=cost(2 * m * width * 3 * head_width, 2 * 3 * width * head_width),
    )(*slots, weight)


def attend_kernel(n_queries, n_pairs, start, end, skip, *refs):
    queries = refs[:n_queries]
    pairs = refs[n_queries : n_queries + n_pairs]
    refs = refs[n_queries + n_pairs :]
    if not start:
        top_in, total_in, mixed_in = refs[:3]
        refs = refs[3:]
    if end:
        out = refs[0]
        refs = refs[1:]
    else:
        top_out, total_out, mixed_out = refs[:3]
        refs = refs[3:]
    q_all, kv_all, sems = refs
    tile, head_width = queries[0].shape
    rows = pairs[0].shape[0]
    copy_all(
        [
            pltpu.make_async_copy(ref, kv_all.at[pl.ds(i * rows, rows), :], sems.at[i])
            for i, ref in enumerate(pairs)
        ]
    )
    keys = n_pairs * rows
    step = 4 * rows

    for i, chunk in enumerate(queries):
        q_all[i * tile : (i + 1) * tile, :] = chunk[...]

    @pl.loop(0, n_queries)
    def _(i):
        here = pl.ds(pl.multiple_of(i * tile, tile), tile)
        there = pl.ds(pl.multiple_of((skip + i) * tile, tile), tile)
        for head in range(head_width // HEAD_DIM):
            columns = slice(head * HEAD_DIM, (head + 1) * HEAD_DIM)
            values = slice(head_width + head * HEAD_DIM, head_width + (head + 1) * HEAD_DIM)
            query = q_all[here, columns]
            scores = [
                lax.dot_general(
                    query,
                    kv_all[k : k + step, columns],
                    (((1,), (1,)), ((), ())),
                    preferred_element_type=jnp.float32,
                )
                for k in range(0, keys, step)
            ]
            top = functools.reduce(jnp.maximum, [jnp.max(s, axis=1, keepdims=True) for s in scores])
            if start:
                total = jnp.zeros((tile, 1), jnp.float32)
                mixed = jnp.zeros((tile, HEAD_DIM), jnp.float32)
            else:
                before = top_in[there, head * HEAD_DIM : head * HEAD_DIM + 1]
                top = jnp.maximum(top, before)
                factor = jnp.exp2((before - top) * EXP2_SCALE)
                total = total_in[there, head * HEAD_DIM : head * HEAD_DIM + 1] * factor
                mixed = mixed_in[there, columns] * factor
            for j, s in enumerate(scores):
                weights = jnp.exp2((s - top) * EXP2_SCALE)
                total = total + jnp.sum(weights, axis=1, keepdims=True)
                mixed = mixed + jnp.dot(
                    weights.astype(jnp.bfloat16),
                    kv_all[j * step : (j + 1) * step, values],
                    preferred_element_type=jnp.float32,
                )
            if end:
                out[here, columns] = (mixed / total).astype(jnp.bfloat16)
            else:
                top_out[here, columns] = jnp.broadcast_to(top, (tile, HEAD_DIM))
                total_out[here, columns] = jnp.broadcast_to(total, (tile, HEAD_DIM))
                mixed_out[here, columns] = mixed


def attend(queries, pairs, state=(), end=False, skip=0):
    m, head_width = queries[0].shape
    rows = pairs[0].shape[0]
    keys = len(pairs) * rows
    n = len(queries)
    whole = jax.ShapeDtypeStruct((n * m, head_width), jnp.float32)
    out_shape = jax.ShapeDtypeStruct((n * m, head_width), jnp.bfloat16) if end else [whole] * 3
    work = n * m * keys * head_width
    return pl.pallas_call(
        functools.partial(attend_kernel, n, len(pairs), not state, end, skip),
        in_specs=[VMEM] * n + [ANY] * len(pairs) + [VMEM] * len(state),
        out_specs=VMEM if end else [VMEM] * 3,
        out_shape=out_shape,
        scratch_shapes=[
            pltpu.VMEM((n * m, head_width), jnp.bfloat16),
            pltpu.VMEM((keys, 2 * head_width), jnp.bfloat16),
            pltpu.SemaphoreType.DMA((len(pairs),)),
        ],
        compiler_params=params(16),
        cost_estimate=cost(4 * work, 4 * keys * head_width),
    )(*queries, *pairs, *state)


def mix_kernel(attended, weight, own, first, other, far):
    n = own.shape[0]
    result = jnp.dot(attended[...], weight[...], preferred_element_type=jnp.float32)
    own[...] = result[:n]
    first[...] = result[n : 2 * n]
    other[...] = result[2 * n : 3 * n].astype(jnp.bfloat16)
    far[...] = result[3 * n :].astype(jnp.bfloat16)


def mix(attended, weight):
    n = attended.shape[0] // 4
    width = weight.shape[1]
    wide = jax.ShapeDtypeStruct((n, width), jnp.float32)
    narrow = jax.ShapeDtypeStruct((n, width), jnp.bfloat16)
    return pl.pallas_call(
        mix_kernel,
        in_specs=[VMEM] * 2,
        out_specs=[VMEM] * 4,
        out_shape=[wide, wide, narrow, narrow],
        compiler_params=params(12),
        cost_estimate=cost(8 * n * attended.shape[1] * width, 2 * attended.shape[1] * width),
    )(attended, weight)


def on_device(tokens, qkv_weight, out_weight):
    rows = tokens.shape[0]
    half = rows // 2
    weight = jnp.transpose(qkv_weight, (1, 0, 2))
    core = lax.axis_index("blk") % CORE

    def pass_last(own_pairs, two_on):
        return send(jnp.where(core == 1, own_pairs, two_on), last_group)

    chunk0, chunk1 = tokens[:half], tokens[half:]
    chunk2 = send(chunk0, across_z)
    first0, other0 = send(chunk0, first_way), send(chunk0, other_way)
    first1, other1 = send(chunk1, first_way), send(chunk1, other_way)
    chunk3 = send(after(chunk1, first0), across_z)
    far0, far1 = send(first0, first_way), send(first1, first_way)
    queries0, pairs0 = project((after(chunk0, chunk2, other1, far1), first0, other0, far0), weight)
    two0 = send(pairs0, chip_before)
    first2, other2 = send(chunk2, first_way), send(chunk2, other_way)
    queries1, pairs1 = project((after(chunk1, pairs0), first1, other1, far1), weight)
    two1 = send(pairs1, chip_before)

    far2 = send(after(first2, pairs1), first_way)
    first3, other3 = send(after(chunk3, pairs1), first_way), send(after(chunk3, pairs1), other_way)
    queries2, pairs2 = project((after(chunk2, chunk3), first2, other2, far2), weight)
    last0 = pass_last(pairs0, two0)
    swapped0 = send(two0, other_core)
    two2 = send(after(pairs2, last0), chip_before)

    far3 = send(after(first3, pairs2), first_way)
    last1 = pass_last(pairs1, two1)
    swapped1 = send(two1, other_core)
    queries3, pairs3 = project((chunk3, first3, other3, far3), weight)
    two3 = send(after(pairs3, last1), chip_before)

    queries = [queries0, queries1, queries2, queries3]
    state = attend(queries, [pairs0, two0, swapped0, last0, pairs1, two1, swapped1, last1])
    last2 = pass_last(pairs2, two2)
    swapped2 = send(two2, other_core)
    two3 = after(two3, state[0], last2)
    last3 = pass_last(pairs3, two3)
    swapped3 = send(two3, other_core)
    state = attend(queries, [pairs2, two2, swapped2, last2], state)
    pairs = [pairs3, two3, swapped3, last3]

    m = 4 * half
    theirs = attend(queries[2:], pairs, state, end=True, skip=2)
    ours = attend(queries[:2], pairs, state, end=True)

    def begin(attended, *earlier):
        own, first, other, far = mix(after(attended, *earlier), out_weight)
        return own, first, send(far, other_way), send(other, first_way)

    def finish(own, first, from_far, from_other, *earlier):
        first = (first + from_far.astype(jnp.float32)).astype(jnp.bfloat16)
        return own + from_other.astype(jnp.float32) + send(after(first, *earlier), other_way).astype(jnp.float32)

    begun2 = begin(theirs[:m])
    begun3 = begin(theirs[m:], begun2[2], begun2[3])
    leaving2 = finish(*begun2).astype(jnp.bfloat16)
    crossed2 = send(leaving2, across_z)
    begun0 = begin(ours[:m], begun3[2], begun3[3], leaving2)
    leaving3 = finish(*begun3).astype(jnp.bfloat16)
    crossed3 = send(leaving3, across_z)
    begun1 = begin(ours[m:], begun0[2], begun0[3], leaving3)
    kept0 = finish(*begun0)
    kept1 = finish(*begun1, crossed2)
    outputs = [
        (kept + crossed.astype(jnp.float32)).astype(jnp.bfloat16)
        for kept, crossed in ((kept0, crossed2), (kept1, crossed3))
    ]
    return jnp.concatenate(outputs, axis=0)


def solution(mesh):
    in_specs = (P(("blk", "uly"), None), P(None, None, "uly"), P("uly", None))
    out_specs = P(("blk", "uly"), None)
    return jax.shard_map(
        on_device, mesh=mesh, in_specs=in_specs, out_specs=out_specs, check_vma=False
    )
```

```python
import functools
import math

import jax
import jax.numpy as jnp
from jax import lax
from jax.experimental import pallas as pl
from jax.experimental.pallas import tpu as pltpu
from jax.sharding import PartitionSpec as P

HEAD_DIM = 128
Z_LO, Y, CORE, Z_HI, X = 4, 4, 2, 2, 4
BOTH = ("blk", "uly")
EXP2_SCALE = math.log2(math.e) / math.sqrt(HEAD_DIM)


def route(move):
    pairs = []
    for place in range(Z_LO * Y * CORE * Z_HI * X):
        blk, uly = divmod(place, Z_HI * X)
        chip, core = divmod(blk, CORE)
        z_hi, x = divmod(uly, X)
        target = move(chip, core, z_hi, x)
        if target is not None:
            chip2, core2, z_hi2, x2 = target
            blk2 = (chip2 % (Z_LO * Y)) * CORE + core2
            pairs.append((place, blk2 * Z_HI * X + (z_hi2 % Z_HI) * X + x2 % X))
    return pairs


def send(block, move):
    return lax.ppermute(block, BOTH, route(move))


def first_way(chip, core, z_hi, x):
    return chip, core, z_hi, x + (1 if core == 0 else -1)


def other_way(chip, core, z_hi, x):
    return chip, core, z_hi, x - (1 if core == 0 else -1)


def across_z(chip, core, z_hi, x):
    return chip, core, z_hi + 1, x


def other_core(chip, core, z_hi, x):
    return chip, 1 - core, z_hi, x


def chip_before(chip, core, z_hi, x):
    return chip - 1, core, z_hi, x


def last_group(chip, core, z_hi, x):
    return (chip, 0, z_hi, x) if core == 1 else (chip - 1, 1, z_hi, x)


def after(block, *earlier):
    return lax.optimization_barrier((block,) + earlier)[0]


VMEM = pl.BlockSpec(memory_space=pltpu.VMEM)
ANY = pl.BlockSpec(memory_space=pl.ANY)


def params(mebibytes):
    return pltpu.CompilerParams(vmem_limit_bytes=mebibytes * 1024 * 1024)


def cost(flops, reads):
    return pl.CostEstimate(flops=flops, bytes_accessed=reads, transcendentals=0)


def copy_all(copies):
    for copy in copies:
        copy.start()
    for copy in copies:
        copy.wait()


def project_kernel(pieces, own, first, other, far, weight, queries, pairs, rows, held, sems):
    n = own.shape[0]
    depth, head_width = weight.shape[1:]
    piece = depth // pieces
    loads = []
    for i, part in enumerate((1, 2, 0)):
        for k in range(pieces):
            source = weight.at[part, pl.ds(k * piece, piece), :]
            at = i * pieces + k
            loads.append(pltpu.make_async_copy(source, held.at[at], sems.at[at]))
    for load in loads:
        load.start()
    for slot, ref in enumerate((own, first, other, far)):
        rows[slot * n : (slot + 1) * n, :] = ref[...]
    for i in range(3):
        total = jnp.zeros((4 * n, head_width), jnp.float32)
        for k in range(pieces):
            at = i * pieces + k
            loads[at].wait()
            total = total + jnp.dot(
                rows[:, k * piece : (k + 1) * piece], held[at], preferred_element_type=jnp.float32
            )
        if i < 2:
            pairs[:, i * head_width : (i + 1) * head_width] = total.astype(jnp.bfloat16)
        else:
            queries[...] = total.astype(jnp.bfloat16)


def project(slots, weight):
    n, width = slots[0].shape
    head_width = weight.shape[2]
    m = 4 * n
    pieces = 2
    return pl.pallas_call(
        functools.partial(project_kernel, pieces),
        in_specs=[VMEM] * 4 + [ANY],
        out_specs=[VMEM] * 2,
        out_shape=[
            jax.ShapeDtypeStruct((m, head_width), jnp.bfloat16),
            jax.ShapeDtypeStruct((m, 2 * head_width), jnp.bfloat16),
        ],
        scratch_shapes=[
            pltpu.VMEM((m, width), jnp.bfloat16),
            pltpu.VMEM((3 * pieces, width // pieces, head_width), jnp.bfloat16),
            pltpu.SemaphoreType.DMA((3 * pieces,)),
        ],
        compiler_params=params(48),
        cost_estimate=cost(2 * m * width * 3 * head_width, 2 * 3 * width * head_width),
    )(*slots, weight)


def attend_kernel(n_queries, n_pairs, start, end, skip, *refs):
    queries = refs[:n_queries]
    pairs = refs[n_queries : n_queries + n_pairs]
    refs = refs[n_queries + n_pairs :]
    if not start:
        top_in, total_in, mixed_in = refs[:3]
        refs = refs[3:]
    if end:
        out = refs[0]
        refs = refs[1:]
    else:
        top_out, total_out, mixed_out = refs[:3]
        refs = refs[3:]
    q_all, kv_all, sems = refs
    tile, head_width = queries[0].shape
    rows = pairs[0].shape[0]
    copy_all(
        [
            pltpu.make_async_copy(ref, kv_all.at[pl.ds(i * rows, rows), :], sems.at[i])
            for i, ref in enumerate(pairs)
        ]
    )
    keys = n_pairs * rows
    step = 4 * rows

    for i, chunk in enumerate(queries):
        q_all[i * tile : (i + 1) * tile, :] = chunk[...]

    @pl.loop(0, n_queries)
    def _(i):
        here = pl.ds(pl.multiple_of(i * tile, tile), tile)
        there = pl.ds(pl.multiple_of((skip + i) * tile, tile), tile)
        for head in range(head_width // HEAD_DIM):
            columns = slice(head * HEAD_DIM, (head + 1) * HEAD_DIM)
            values = slice(head_width + head * HEAD_DIM, head_width + (head + 1) * HEAD_DIM)
            query = q_all[here, columns]
            scores = [
                lax.dot_general(
                    query,
                    kv_all[k : k + step, columns],
                    (((1,), (1,)), ((), ())),
                    preferred_element_type=jnp.float32,
                )
                for k in range(0, keys, step)
            ]
            top = functools.reduce(jnp.maximum, [jnp.max(s, axis=1, keepdims=True) for s in scores])
            if start:
                total = jnp.zeros((tile, 1), jnp.float32)
                mixed = jnp.zeros((tile, HEAD_DIM), jnp.float32)
            else:
                before = top_in[there, head * HEAD_DIM : head * HEAD_DIM + 1]
                top = jnp.maximum(top, before)
                factor = jnp.exp2((before - top) * EXP2_SCALE)
                total = total_in[there, head * HEAD_DIM : head * HEAD_DIM + 1] * factor
                mixed = mixed_in[there, columns] * factor
            for j, s in enumerate(scores):
                weights = jnp.exp2((s - top) * EXP2_SCALE)
                total = total + jnp.sum(weights, axis=1, keepdims=True)
                mixed = mixed + jnp.dot(
                    weights.astype(jnp.bfloat16),
                    kv_all[j * step : (j + 1) * step, values],
                    preferred_element_type=jnp.float32,
                )
            if end:
                out[here, columns] = (mixed / total).astype(jnp.bfloat16)
            else:
                top_out[here, columns] = jnp.broadcast_to(top, (tile, HEAD_DIM))
                total_out[here, columns] = jnp.broadcast_to(total, (tile, HEAD_DIM))
                mixed_out[here, columns] = mixed


def attend(queries, pairs, state=(), end=False, skip=0):
    m, head_width = queries[0].shape
    rows = pairs[0].shape[0]
    keys = len(pairs) * rows
    n = len(queries)
    whole = jax.ShapeDtypeStruct((n * m, head_width), jnp.float32)
    out_shape = jax.ShapeDtypeStruct((n * m, head_width), jnp.bfloat16) if end else [whole] * 3
    work = n * m * keys * head_width
    return pl.pallas_call(
        functools.partial(attend_kernel, n, len(pairs), not state, end, skip),
        in_specs=[VMEM] * n + [ANY] * len(pairs) + [VMEM] * len(state),
        out_specs=VMEM if end else [VMEM] * 3,
        out_shape=out_shape,
        scratch_shapes=[
            pltpu.VMEM((n * m, head_width), jnp.bfloat16),
            pltpu.VMEM((keys, 2 * head_width), jnp.bfloat16),
            pltpu.SemaphoreType.DMA((len(pairs),)),
        ],
        compiler_params=params(16),
        cost_estimate=cost(4 * work, 4 * keys * head_width),
    )(*queries, *pairs, *state)


def mix_kernel(attended, weight, own, first, other, far):
    n = own.shape[0]
    result = jnp.dot(attended[...], weight[...], preferred_element_type=jnp.float32)
    own[...] = result[:n]
    first[...] = result[n : 2 * n]
    other[...] = result[2 * n : 3 * n].astype(jnp.bfloat16)
    far[...] = result[3 * n :].astype(jnp.bfloat16)


def mix(attended, weight):
    n = attended.shape[0] // 4
    width = weight.shape[1]
    wide = jax.ShapeDtypeStruct((n, width), jnp.float32)
    narrow = jax.ShapeDtypeStruct((n, width), jnp.bfloat16)
    return pl.pallas_call(
        mix_kernel,
        in_specs=[VMEM] * 2,
        out_specs=[VMEM] * 4,
        out_shape=[wide, wide, narrow, narrow],
        compiler_params=params(12),
        cost_estimate=cost(8 * n * attended.shape[1] * width, 2 * attended.shape[1] * width),
    )(attended, weight)


def on_device(tokens, qkv_weight, out_weight):
    rows = tokens.shape[0]
    half = rows // 2
    weight = jnp.transpose(qkv_weight, (1, 0, 2))
    core = lax.axis_index("blk") % CORE

    def pass_last(own_pairs, two_on):
        return send(jnp.where(core == 1, own_pairs, two_on), last_group)

    chunk0, chunk1 = tokens[:half], tokens[half:]
    chunk2 = send(chunk0, across_z)
    first0, other0 = send(chunk0, first_way), send(chunk0, other_way)
    first1, other1 = send(chunk1, first_way), send(chunk1, other_way)
    chunk3 = send(after(chunk1, first0), across_z)
    far0, far1 = send(first0, first_way), send(first1, first_way)
    queries0, pairs0 = project((after(chunk0, chunk2, other1, far1), first0, other0, far0), weight)
    two0 = send(pairs0, chip_before)
    first2, other2 = send(chunk2, first_way), send(chunk2, other_way)
    queries1, pairs1 = project((after(chunk1, pairs0), first1, other1, far1), weight)
    two1 = send(pairs1, chip_before)

    far2 = send(after(first2, pairs1), first_way)
    first3, other3 = send(after(chunk3, pairs1), first_way), send(after(chunk3, pairs1), other_way)
    queries2, pairs2 = project((after(chunk2, chunk3), first2, other2, far2), weight)
    last0 = pass_last(pairs0, two0)
    swapped0 = send(two0, other_core)
    two2 = send(after(pairs2, last0), chip_before)

    far3 = send(after(first3, pairs2), first_way)
    last1 = pass_last(pairs1, two1)
    swapped1 = send(two1, other_core)
    queries3, pairs3 = project((chunk3, first3, other3, far3), weight)
    two3 = send(after(pairs3, last1), chip_before)

    queries = [queries0, queries1, queries2, queries3]
    state = attend(queries, [pairs0, two0, swapped0, last0, pairs1, two1, swapped1, last1])
    last2 = pass_last(pairs2, two2)
    swapped2 = send(two2, other_core)
    two3 = after(two3, state[0], last2)
    last3 = pass_last(pairs3, two3)
    swapped3 = send(two3, other_core)
    pairs = [pairs2, two2, swapped2, last2, pairs3, two3, swapped3, last3]

    m = 4 * half
    theirs = attend(queries[2:], pairs, state, end=True, skip=2)
    ours = attend(queries[:2], pairs, state, end=True)

    def begin(attended, *earlier):
        own, first, other, far = mix(after(attended, *earlier), out_weight)
        return own, first, send(far, other_way), send(other, first_way)

    def finish(own, first, from_far, from_other, *earlier):
        first = (first + from_far.astype(jnp.float32)).astype(jnp.bfloat16)
        return own + from_other.astype(jnp.float32) + send(after(first, *earlier), other_way).astype(jnp.float32)

    begun2 = begin(theirs[:m])
    begun3 = begin(theirs[m:])
    leaving2 = finish(*begun2).astype(jnp.bfloat16)
    crossed2 = send(leaving2, across_z)
    begun0 = begin(ours[:m], begun3[2], begun3[3], leaving2)
    leaving3 = finish(*begun3).astype(jnp.bfloat16)
    crossed3 = send(leaving3, across_z)
    begun1 = begin(ours[m:], leaving3)
    kept0 = finish(*begun0)
    kept1 = finish(*begun1)
    outputs = [
        (kept + crossed.astype(jnp.float32)).astype(jnp.bfloat16)
        for kept, crossed in ((kept0, crossed2), (kept1, crossed3))
    ]
    return jnp.concatenate(outputs, axis=0)


def solution(mesh):
    in_specs = (P(("blk", "uly"), None), P(None, None, "uly"), P("uly", None))
    out_specs = P(("blk", "uly"), None)
    return jax.shard_map(
        on_device, mesh=mesh, in_specs=in_specs, out_specs=out_specs, check_vma=False
    )
```

```python
import functools
import math

import jax
import jax.numpy as jnp
from jax import lax
from jax.experimental import pallas as pl
from jax.experimental.pallas import tpu as pltpu
from jax.sharding import PartitionSpec as P

HEAD_DIM = 128
Z_LO, Y, CORE, Z_HI, X = 4, 4, 2, 2, 4
BOTH = ("blk", "uly")
TILE, STEP = 384, 768
EXP2_SCALE = math.log2(math.e) / math.sqrt(HEAD_DIM)


def route(move):
    pairs = []
    for place in range(Z_LO * Y * CORE * Z_HI * X):
        blk, uly = divmod(place, Z_HI * X)
        chip, core = divmod(blk, CORE)
        z_hi, x = divmod(uly, X)
        target = move(chip, core, z_hi, x)
        if target is not None:
            chip2, core2, z_hi2, x2 = target
            blk2 = (chip2 % (Z_LO * Y)) * CORE + core2
            pairs.append((place, blk2 * Z_HI * X + (z_hi2 % Z_HI) * X + x2 % X))
    return pairs


def send(block, move):
    return lax.ppermute(block, BOTH, route(move))


def first_way(chip, core, z_hi, x):
    return chip, core, z_hi, x + (1 if core == 0 else -1)


def other_way(chip, core, z_hi, x):
    return chip, core, z_hi, x - (1 if core == 0 else -1)


def half_way(chip, core, z_hi, x):
    return chip, core, z_hi, x + 2


def across_z(chip, core, z_hi, x):
    return chip, core, z_hi + 1, x


def other_core(chip, core, z_hi, x):
    return chip, 1 - core, z_hi, x


def chip_before(chip, core, z_hi, x):
    return chip - 1, core, z_hi, x


def last_group(chip, core, z_hi, x):
    return (chip, 0, z_hi, x) if core == 1 else (chip - 1, 1, z_hi, x)


def after(block, *earlier):
    return lax.optimization_barrier((block,) + earlier)[0]


VMEM = pl.BlockSpec(memory_space=pltpu.VMEM)
ANY = pl.BlockSpec(memory_space=pl.ANY)


def params(mebibytes):
    return pltpu.CompilerParams(vmem_limit_bytes=mebibytes * 1024 * 1024)


def cost(flops, reads):
    return pl.CostEstimate(flops=flops, bytes_accessed=reads, transcendentals=0)


def copy_all(copies):
    for copy in copies:
        copy.start()
    for copy in copies:
        copy.wait()


def project_kernel(pieces, own, first, other, far, weight, queries, pairs, rows, held, sems):
    n = own.shape[0]
    depth, head_width = weight.shape[1:]
    piece = depth // pieces
    loads = []
    for i, part in enumerate((1, 2, 0)):
        for k in range(pieces):
            source = weight.at[part, pl.ds(k * piece, piece), :]
            at = i * pieces + k
            loads.append(pltpu.make_async_copy(source, held.at[at], sems.at[at]))
    for load in loads:
        load.start()
    for slot, ref in enumerate((own, first, other, far)):
        rows[slot * n : (slot + 1) * n, :] = ref[...]
    for i in range(3):
        total = jnp.zeros((4 * n, head_width), jnp.float32)
        for k in range(pieces):
            at = i * pieces + k
            loads[at].wait()
            total = total + jnp.dot(
                rows[:, k * piece : (k + 1) * piece], held[at], preferred_element_type=jnp.float32
            )
        if i < 2:
            pairs[:, i * head_width : (i + 1) * head_width] = total.astype(jnp.bfloat16)
        else:
            queries[...] = total.astype(jnp.bfloat16)


def project(slots, weight):
    n, width = slots[0].shape
    head_width = weight.shape[2]
    m = 4 * n
    pieces = 2
    return pl.pallas_call(
        functools.partial(project_kernel, pieces),
        in_specs=[VMEM] * 4 + [ANY],
        out_specs=[VMEM] * 2,
        out_shape=[
            jax.ShapeDtypeStruct((m, head_width), jnp.bfloat16),
            jax.ShapeDtypeStruct((m, 2 * head_width), jnp.bfloat16),
        ],
        scratch_shapes=[
            pltpu.VMEM((m, width), jnp.bfloat16),
            pltpu.VMEM((3 * pieces, width // pieces, head_width), jnp.bfloat16),
            pltpu.SemaphoreType.DMA((3 * pieces,)),
        ],
        compiler_params=params(48),
        cost_estimate=cost(2 * m * width * 3 * head_width, 2 * 3 * width * head_width),
    )(*slots, weight)


def attend_kernel(n_queries, n_pairs, start, end, skip, *refs):
    queries = refs[:n_queries]
    pairs = refs[n_queries : n_queries + n_pairs]
    refs = refs[n_queries + n_pairs :]
    if not start:
        top_in, total_in, mixed_in = refs[:3]
        refs = refs[3:]
    if end:
        out = refs[0]
        refs = refs[1:]
    else:
        top_out, total_out, mixed_out = refs[:3]
        refs = refs[3:]
    q_all, kv_all, sems = refs
    head_width = q_all.shape[1]
    heads = head_width // HEAD_DIM
    copies = []
    at = 0
    for i, ref in enumerate(pairs):
        copies.append(pltpu.make_async_copy(ref, kv_all.at[pl.ds(at, ref.shape[0]), :], sems.at[i]))
        at += ref.shape[0]
    for copy in copies:
        copy.start()
    at = 0
    for ref in queries:
        q_all[at : at + ref.shape[0], :] = ref[...]
        at += ref.shape[0]
    for copy in copies:
        copy.wait()
    keys = kv_all.shape[0]

    @pl.loop(0, q_all.shape[0] // TILE)
    def _(i):
        here = pl.ds(pl.multiple_of(i * TILE, TILE), TILE)
        there = pl.ds(pl.multiple_of(skip + i * TILE, TILE), TILE)

        def score(head):
            columns = slice(head * HEAD_DIM, (head + 1) * HEAD_DIM)
            return [
                lax.dot_general(
                    q_all[here, columns],
                    kv_all[k : k + STEP, columns],
                    (((1,), (1,)), ((), ())),
                    preferred_element_type=jnp.float32,
                )
                for k in range(0, keys, STEP)
            ]

        scores = score(0)
        for head in range(heads):
            later = score(head + 1) if head + 1 < heads else None
            columns = slice(head * HEAD_DIM, (head + 1) * HEAD_DIM)
            values = slice(head_width + head * HEAD_DIM, head_width + (head + 1) * HEAD_DIM)
            top = functools.reduce(jnp.maximum, [jnp.max(s, axis=1, keepdims=True) for s in scores])
            if start:
                total = jnp.zeros((TILE, 1), jnp.float32)
                mixed = jnp.zeros((TILE, HEAD_DIM), jnp.float32)
            else:
                before = top_in[there, head * HEAD_DIM : head * HEAD_DIM + 1]
                top = jnp.maximum(top, before)
                factor = jnp.exp2((before - top) * EXP2_SCALE)
                total = total_in[there, head * HEAD_DIM : head * HEAD_DIM + 1] * factor
                mixed = mixed_in[there, columns] * factor
            for j, s in enumerate(scores):
                weights = jnp.exp2((s - top) * EXP2_SCALE)
                total = total + jnp.sum(weights, axis=1, keepdims=True)
                mixed = mixed + jnp.dot(
                    weights.astype(jnp.bfloat16),
                    kv_all[j * STEP : (j + 1) * STEP, values],
                    preferred_element_type=jnp.float32,
                )
            if end:
                out[here, columns] = (mixed / total).astype(jnp.bfloat16)
            else:
                top_out[here, columns] = jnp.broadcast_to(top, (TILE, HEAD_DIM))
                total_out[here, columns] = jnp.broadcast_to(total, (TILE, HEAD_DIM))
                mixed_out[here, columns] = mixed
            scores = later


def attend(queries, pairs, state=(), end=False, skip=0):
    head_width = queries[0].shape[1]
    m = sum(q.shape[0] for q in queries)
    keys = sum(p.shape[0] for p in pairs)
    whole = jax.ShapeDtypeStruct((m, head_width), jnp.float32)
    out_shape = jax.ShapeDtypeStruct((m, head_width), jnp.bfloat16) if end else [whole] * 3
    return pl.pallas_call(
        functools.partial(attend_kernel, len(queries), len(pairs), not state, end, skip),
        in_specs=[VMEM] * len(queries) + [ANY] * len(pairs) + [VMEM] * len(state),
        out_specs=VMEM if end else [VMEM] * 3,
        out_shape=out_shape,
        scratch_shapes=[
            pltpu.VMEM((m, head_width), jnp.bfloat16),
            pltpu.VMEM((keys, 2 * head_width), jnp.bfloat16),
            pltpu.SemaphoreType.DMA((len(pairs),)),
        ],
        compiler_params=params(20),
        cost_estimate=cost(4 * m * keys * head_width, 4 * keys * head_width),
    )(*queries, *pairs, *state)


def mix_kernel(attended, weight, own, first, other, far):
    n = own.shape[0]
    result = jnp.dot(attended[...], weight[...], preferred_element_type=jnp.float32)
    own[...] = result[:n]
    first[...] = result[n : 2 * n].astype(first.dtype)
    other[...] = result[2 * n : 3 * n].astype(jnp.bfloat16)
    far[...] = result[3 * n :].astype(jnp.bfloat16)


def mix(attended, weight, first_type):
    n = attended.shape[0] // 4
    width = weight.shape[1]
    wide = jax.ShapeDtypeStruct((n, width), jnp.float32)
    narrow = jax.ShapeDtypeStruct((n, width), jnp.bfloat16)
    return pl.pallas_call(
        mix_kernel,
        in_specs=[VMEM] * 2,
        out_specs=[VMEM] * 4,
        out_shape=[wide, jax.ShapeDtypeStruct((n, width), first_type), narrow, narrow],
        compiler_params=params(12),
        cost_estimate=cost(8 * n * attended.shape[1] * width, 2 * attended.shape[1] * width),
    )(attended, weight)


def on_device(tokens, qkv_weight, out_weight):
    rows = tokens.shape[0]
    half = rows // 2
    weight = jnp.transpose(qkv_weight, (1, 0, 2))
    core = lax.axis_index("blk") % CORE

    def pass_last(own_pairs, two_on):
        return send(jnp.where(core == 1, own_pairs, two_on), last_group)

    chunk0, chunk1 = tokens[:half], tokens[half:]
    chunk2 = send(chunk0, across_z)
    first0, other0 = send(chunk0, first_way), send(chunk0, other_way)
    first1, other1 = send(chunk1, first_way), send(chunk1, other_way)
    chunk3 = send(after(chunk1, first0), across_z)
    far0, far1 = send(first0, first_way), send(first1, first_way)
    queries0, pairs0 = project((after(chunk0, chunk2, other1, far1), first0, other0, far0), weight)
    two0 = send(pairs0, chip_before)
    first2, other2 = send(chunk2, first_way), send(chunk2, other_way)
    queries1, pairs1 = project((after(chunk1, pairs0), first1, other1, far1), weight)
    two1 = send(pairs1, chip_before)

    far2 = send(after(first2, pairs1), first_way)
    first3, other3 = send(after(chunk3, pairs1), first_way), send(after(chunk3, pairs1), other_way)
    queries2, pairs2 = project((after(chunk2, chunk3), first2, other2, far2), weight)
    last0 = pass_last(pairs0, two0)
    swapped0 = send(two0, other_core)
    two2 = send(after(pairs2, last0), chip_before)

    far3 = send(after(first3, pairs2), first_way)
    last1 = pass_last(pairs1, two1)
    swapped1 = send(two1, other_core)
    queries3, pairs3 = project((chunk3, first3, other3, far3), weight)
    two3 = send(after(pairs3, last1), chip_before)

    queries = [queries0, queries1, queries2, queries3]
    state = attend(queries, [pairs0, two0, swapped0, last0, pairs1, two1, swapped1, last1])
    last2 = pass_last(pairs2, two2)
    swapped2 = send(two2, other_core)
    two3 = after(two3, state[0], last2)
    last3 = pass_last(pairs3, two3)
    swapped3 = send(two3, other_core)
    pairs = [pairs2, two2, swapped2, last2, pairs3, two3, swapped3, last3]

    m = 4 * half
    theirs = attend(queries[2:], pairs, state, end=True, skip=2 * m)
    ours = attend(queries[:2], pairs, state, end=True)

    def begin(attended, *earlier):
        own, first, other, far = mix(after(attended, *earlier), out_weight, jnp.float32)
        return own, first, send(far, other_way), send(other, first_way)

    def finish(own, first, from_far, from_other, *earlier):
        first = (first + from_far.astype(jnp.float32)).astype(jnp.bfloat16)
        return own + from_other.astype(jnp.float32) + send(after(first, *earlier), other_way).astype(jnp.float32)

    own, first, other, far = mix(theirs[:m], out_weight, jnp.bfloat16)
    arriving = [send(far, half_way), send(first, other_way), send(other, first_way)]
    begun3 = begin(theirs[m:])
    leaving2 = (after(own, ours) + sum(part.astype(jnp.float32) for part in arriving)).astype(jnp.bfloat16)
    crossed2 = send(leaving2, across_z)
    begun0 = begin(ours[:m], begun3[2], begun3[3], leaving2)
    leaving3 = finish(*begun3, leaving2).astype(jnp.bfloat16)
    crossed3 = send(leaving3, across_z)
    begun1 = begin(ours[m:], leaving3)
    kept0 = finish(*begun0)
    kept1 = finish(*begun1)
    outputs = [
        (kept + crossed.astype(jnp.float32)).astype(jnp.bfloat16)
        for kept, crossed in ((kept0, crossed2), (kept1, crossed3))
    ]
    return jnp.concatenate(outputs, axis=0)


def solution(mesh):
    in_specs = (P(("blk", "uly"), None), P(None, None, "uly"), P("uly", None))
    out_specs = P(("blk", "uly"), None)
    return jax.shard_map(
        on_device, mesh=mesh, in_specs=in_specs, out_specs=out_specs, check_vma=False
    )
```

```python
import functools
import math

import jax
import jax.numpy as jnp
from jax import lax
from jax.experimental import pallas as pl
from jax.experimental.pallas import tpu as pltpu
from jax.sharding import PartitionSpec as P

HEAD_DIM = 128
Z_LO, Y, CORE, Z_HI, X = 4, 4, 2, 2, 4
BOTH = ("blk", "uly")
TILE, STEP = 384, 768
EXP2_SCALE = math.log2(math.e) / math.sqrt(HEAD_DIM)


def route(move):
    pairs = []
    for place in range(Z_LO * Y * CORE * Z_HI * X):
        blk, uly = divmod(place, Z_HI * X)
        chip, core = divmod(blk, CORE)
        z_hi, x = divmod(uly, X)
        target = move(chip, core, z_hi, x)
        if target is not None:
            chip2, core2, z_hi2, x2 = target
            blk2 = (chip2 % (Z_LO * Y)) * CORE + core2
            pairs.append((place, blk2 * Z_HI * X + (z_hi2 % Z_HI) * X + x2 % X))
    return pairs


def send(block, move):
    return lax.ppermute(block, BOTH, route(move))


def first_way(chip, core, z_hi, x):
    return chip, core, z_hi, x + (1 if core == 0 else -1)


def other_way(chip, core, z_hi, x):
    return chip, core, z_hi, x - (1 if core == 0 else -1)


def half_way(chip, core, z_hi, x):
    return chip, core, z_hi, x + 2


def across_z(chip, core, z_hi, x):
    return chip, core, z_hi + 1, x


def other_core(chip, core, z_hi, x):
    return chip, 1 - core, z_hi, x


def chip_before(chip, core, z_hi, x):
    return chip - 1, core, z_hi, x


def last_group(chip, core, z_hi, x):
    return (chip, 0, z_hi, x) if core == 1 else (chip - 1, 1, z_hi, x)


def after(block, *earlier):
    return lax.optimization_barrier((block,) + earlier)[0]


VMEM = pl.BlockSpec(memory_space=pltpu.VMEM)
ANY = pl.BlockSpec(memory_space=pl.ANY)


def params(mebibytes):
    return pltpu.CompilerParams(vmem_limit_bytes=mebibytes * 1024 * 1024)


def cost(flops, reads):
    return pl.CostEstimate(flops=flops, bytes_accessed=reads, transcendentals=0)


def copy_all(copies):
    for copy in copies:
        copy.start()
    for copy in copies:
        copy.wait()


def project_kernel(pieces, n_slots, *refs):
    slots = refs[:n_slots]
    weight, queries = refs[n_slots : n_slots + 2]
    pairs = refs[n_slots + 2 : -3]
    rows, held, sems = refs[-3:]
    n = slots[0].shape[0]
    depth, head_width = weight.shape[1:]
    piece = depth // pieces
    loads = []
    for i, part in enumerate((1, 2, 0)):
        for k in range(pieces):
            source = weight.at[part, pl.ds(k * piece, piece), :]
            at = i * pieces + k
            loads.append(pltpu.make_async_copy(source, held.at[at], sems.at[at]))
    for load in loads:
        load.start()
    for slot, ref in enumerate(slots):
        rows[slot * n : (slot + 1) * n, :] = ref[...]
    for i in range(3):
        total = jnp.zeros((n_slots * n, head_width), jnp.float32)
        for k in range(pieces):
            at = i * pieces + k
            loads[at].wait()
            total = total + jnp.dot(
                rows[:, k * piece : (k + 1) * piece], held[at], preferred_element_type=jnp.float32
            )
        result = total.astype(jnp.bfloat16)
        if i < 2:
            for j, ref in enumerate(pairs):
                ref[:, i * head_width : (i + 1) * head_width] = result[j * 4 * n : (j + 1) * 4 * n]
        else:
            queries[...] = result


def project(chunks, weight):
    slots = sum(chunks, ())
    n, width = slots[0].shape
    head_width = weight.shape[2]
    m = len(slots) * n
    pieces = 2
    return pl.pallas_call(
        functools.partial(project_kernel, pieces, len(slots)),
        in_specs=[VMEM] * len(slots) + [ANY],
        out_specs=[VMEM] * (1 + len(chunks)),
        out_shape=[jax.ShapeDtypeStruct((m, head_width), jnp.bfloat16)]
        + [jax.ShapeDtypeStruct((4 * n, 2 * head_width), jnp.bfloat16)] * len(chunks),
        scratch_shapes=[
            pltpu.VMEM((m, width), jnp.bfloat16),
            pltpu.VMEM((3 * pieces, width // pieces, head_width), jnp.bfloat16),
            pltpu.SemaphoreType.DMA((3 * pieces,)),
        ],
        compiler_params=params(48),
        cost_estimate=cost(2 * m * width * 3 * head_width, 2 * 3 * width * head_width),
    )(*slots, weight)


def attend_kernel(n_queries, n_pairs, start, end, skip, *refs):
    queries = refs[:n_queries]
    pairs = refs[n_queries : n_queries + n_pairs]
    refs = refs[n_queries + n_pairs :]
    if not start:
        top_in, total_in, mixed_in = refs[:3]
        refs = refs[3:]
    if end:
        out = refs[0]
        refs = refs[1:]
    else:
        top_out, total_out, mixed_out = refs[:3]
        refs = refs[3:]
    q_all, kv_all, sems = refs
    head_width = q_all.shape[1]
    heads = head_width // HEAD_DIM
    copies = []
    at = 0
    for i, ref in enumerate(pairs):
        copies.append(pltpu.make_async_copy(ref, kv_all.at[pl.ds(at, ref.shape[0]), :], sems.at[i]))
        at += ref.shape[0]
    for copy in copies:
        copy.start()
    at = 0
    for ref in queries:
        q_all[at : at + ref.shape[0], :] = ref[...]
        at += ref.shape[0]
    for copy in copies:
        copy.wait()
    keys = kv_all.shape[0]

    @pl.loop(0, q_all.shape[0] // TILE)
    def _(i):
        here = pl.ds(pl.multiple_of(i * TILE, TILE), TILE)
        there = pl.ds(pl.multiple_of(skip + i * TILE, TILE), TILE)

        def score(head):
            columns = slice(head * HEAD_DIM, (head + 1) * HEAD_DIM)
            return [
                lax.dot_general(
                    q_all[here, columns],
                    kv_all[k : k + STEP, columns],
                    (((1,), (1,)), ((), ())),
                    preferred_element_type=jnp.float32,
                )
                for k in range(0, keys, STEP)
            ]

        scores = score(0)
        for head in range(heads):
            later = score(head + 1) if head + 1 < heads else None
            columns = slice(head * HEAD_DIM, (head + 1) * HEAD_DIM)
            values = slice(head_width + head * HEAD_DIM, head_width + (head + 1) * HEAD_DIM)
            top = functools.reduce(jnp.maximum, [jnp.max(s, axis=1, keepdims=True) for s in scores])
            if start:
                total = jnp.zeros((TILE, 1), jnp.float32)
                mixed = jnp.zeros((TILE, HEAD_DIM), jnp.float32)
            else:
                before = top_in[there, head * HEAD_DIM : head * HEAD_DIM + 1]
                top = jnp.maximum(top, before)
                factor = jnp.exp2((before - top) * EXP2_SCALE)
                total = total_in[there, head * HEAD_DIM : head * HEAD_DIM + 1] * factor
                mixed = mixed_in[there, columns] * factor
            for j, s in enumerate(scores):
                weights = jnp.exp2((s - top) * EXP2_SCALE)
                total = total + jnp.sum(weights, axis=1, keepdims=True)
                mixed = mixed + jnp.dot(
                    weights.astype(jnp.bfloat16),
                    kv_all[j * STEP : (j + 1) * STEP, values],
                    preferred_element_type=jnp.float32,
                )
            if end:
                out[here, columns] = (mixed / total).astype(jnp.bfloat16)
            else:
                top_out[here, columns] = jnp.broadcast_to(top, (TILE, HEAD_DIM))
                total_out[here, columns] = jnp.broadcast_to(total, (TILE, HEAD_DIM))
                mixed_out[here, columns] = mixed
            scores = later


def attend(queries, pairs, state=(), end=False, skip=0):
    head_width = queries[0].shape[1]
    m = sum(q.shape[0] for q in queries)
    keys = sum(p.shape[0] for p in pairs)
    whole = jax.ShapeDtypeStruct((m, head_width), jnp.float32)
    out_shape = jax.ShapeDtypeStruct((m, head_width), jnp.bfloat16) if end else [whole] * 3
    return pl.pallas_call(
        functools.partial(attend_kernel, len(queries), len(pairs), not state, end, skip),
        in_specs=[VMEM] * len(queries) + [ANY] * len(pairs) + [VMEM] * len(state),
        out_specs=VMEM if end else [VMEM] * 3,
        out_shape=out_shape,
        scratch_shapes=[
            pltpu.VMEM((m, head_width), jnp.bfloat16),
            pltpu.VMEM((keys, 2 * head_width), jnp.bfloat16),
            pltpu.SemaphoreType.DMA((len(pairs),)),
        ],
        compiler_params=params(20),
        cost_estimate=cost(4 * m * keys * head_width, 4 * keys * head_width),
    )(*queries, *pairs, *state)


def mix_kernel(attended, weight, own, first, other, far):
    n = own.shape[0]
    result = jnp.dot(attended[...], weight[...], preferred_element_type=jnp.float32)
    own[...] = result[:n]
    first[...] = result[n : 2 * n].astype(first.dtype)
    other[...] = result[2 * n : 3 * n].astype(jnp.bfloat16)
    far[...] = result[3 * n :].astype(jnp.bfloat16)


def mix(attended, weight, first_type):
    n = attended.shape[0] // 4
    width = weight.shape[1]
    wide = jax.ShapeDtypeStruct((n, width), jnp.float32)
    narrow = jax.ShapeDtypeStruct((n, width), jnp.bfloat16)
    return pl.pallas_call(
        mix_kernel,
        in_specs=[VMEM] * 2,
        out_specs=[VMEM] * 4,
        out_shape=[wide, jax.ShapeDtypeStruct((n, width), first_type), narrow, narrow],
        compiler_params=params(12),
        cost_estimate=cost(8 * n * attended.shape[1] * width, 2 * attended.shape[1] * width),
    )(attended, weight)


def on_device(tokens, qkv_weight, out_weight):
    rows = tokens.shape[0]
    half = rows // 2
    weight = jnp.transpose(qkv_weight, (1, 0, 2))
    core = lax.axis_index("blk") % CORE

    def pass_last(own_pairs, two_on):
        return send(jnp.where(core == 1, own_pairs, two_on), last_group)

    chunk0, chunk1 = tokens[:half], tokens[half:]
    chunk2 = send(chunk0, across_z)
    first0, other0 = send(chunk0, first_way), send(chunk0, other_way)
    first1, other1 = send(chunk1, first_way), send(chunk1, other_way)
    chunk3 = send(after(chunk1, first0), across_z)
    far0, far1 = send(first0, first_way), send(first1, first_way)
    first2, other2 = send(chunk2, first_way), send(chunk2, other_way)
    slots0 = (after(chunk0, chunk2, other1, far1), first0, other0, far0)
    queries0, pairs0, pairs1 = project([slots0, (chunk1, first1, other1, far1)], weight)
    two0 = send(pairs0, chip_before)
    two1 = send(pairs1, chip_before)

    far2 = send(after(first2, pairs1), first_way)
    first3, other3 = send(after(chunk3, pairs1), first_way), send(after(chunk3, pairs1), other_way)
    queries2, pairs2 = project([(after(chunk2, chunk3), first2, other2, far2)], weight)
    last0 = pass_last(pairs0, two0)
    swapped0 = send(two0, other_core)
    two2 = send(after(pairs2, last0), chip_before)

    far3 = send(after(first3, pairs2), first_way)
    last1 = pass_last(pairs1, two1)
    swapped1 = send(two1, other_core)
    queries3, pairs3 = project([(chunk3, first3, other3, far3)], weight)
    two3 = send(after(pairs3, last1), chip_before)

    queries = [queries0, queries2, queries3]
    state = attend(queries, [pairs0, two0, swapped0, last0, pairs1, two1, swapped1, last1])
    last2 = pass_last(pairs2, two2)
    swapped2 = send(two2, other_core)
    two3 = after(two3, state[0], last2)
    last3 = pass_last(pairs3, two3)
    swapped3 = send(two3, other_core)
    pairs = [pairs2, two2, swapped2, last2, pairs3, two3, swapped3, last3]

    m = 4 * half
    theirs = attend(queries[1:], pairs, state, end=True, skip=2 * m)
    ours = attend(queries[:1], pairs, state, end=True)

    def begin(attended, *earlier):
        own, first, other, far = mix(after(attended, *earlier), out_weight, jnp.float32)
        return own, first, send(far, other_way), send(other, first_way)

    def finish(own, first, from_far, from_other, *earlier):
        first = (first + from_far.astype(jnp.float32)).astype(jnp.bfloat16)
        return own + from_other.astype(jnp.float32) + send(after(first, *earlier), other_way).astype(jnp.float32)

    own, first, other, far = mix(theirs[:m], out_weight, jnp.bfloat16)
    arriving = [send(far, half_way), send(first, other_way), send(other, first_way)]
    begun3 = begin(theirs[m:])
    leaving2 = (after(own, ours) + sum(part.astype(jnp.float32) for part in arriving)).astype(jnp.bfloat16)
    crossed2 = send(leaving2, across_z)
    begun0 = begin(ours[:m], begun3[2], begun3[3], leaving2)
    leaving3 = finish(*begun3, leaving2).astype(jnp.bfloat16)
    crossed3 = send(leaving3, across_z)
    begun1 = begin(ours[m:], leaving3)
    kept0 = finish(*begun0)
    kept1 = finish(*begun1)
    outputs = [
        (kept + crossed.astype(jnp.float32)).astype(jnp.bfloat16)
        for kept, crossed in ((kept0, crossed2), (kept1, crossed3))
    ]
    return jnp.concatenate(outputs, axis=0)


def solution(mesh):
    in_specs = (P(("blk", "uly"), None), P(None, None, "uly"), P("uly", None))
    out_specs = P(("blk", "uly"), None)
    return jax.shard_map(
        on_device, mesh=mesh, in_specs=in_specs, out_specs=out_specs, check_vma=False
    )
```

```python
import functools
import math

import jax
import jax.numpy as jnp
from jax import lax
from jax.experimental import pallas as pl
from jax.experimental.pallas import tpu as pltpu
from jax.sharding import PartitionSpec as P

HEAD_DIM = 128
Z_LO, Y, CORE, Z_HI, X = 4, 4, 2, 2, 4
BOTH = ("blk", "uly")
TILE, STEP = 384, 768
EXP2_SCALE = math.log2(math.e) / math.sqrt(HEAD_DIM)


def route(move):
    pairs = []
    for place in range(Z_LO * Y * CORE * Z_HI * X):
        blk, uly = divmod(place, Z_HI * X)
        chip, core = divmod(blk, CORE)
        z_hi, x = divmod(uly, X)
        target = move(chip, core, z_hi, x)
        if target is not None:
            chip2, core2, z_hi2, x2 = target
            blk2 = (chip2 % (Z_LO * Y)) * CORE + core2
            pairs.append((place, blk2 * Z_HI * X + (z_hi2 % Z_HI) * X + x2 % X))
    return pairs


def send(block, move):
    return lax.ppermute(block, BOTH, route(move))


def first_way(chip, core, z_hi, x):
    return chip, core, z_hi, x + (1 if core == 0 else -1)


def other_way(chip, core, z_hi, x):
    return chip, core, z_hi, x - (1 if core == 0 else -1)


def half_way(chip, core, z_hi, x):
    return chip, core, z_hi, x + 2


def across_z(chip, core, z_hi, x):
    return chip, core, z_hi + 1, x


def other_core(chip, core, z_hi, x):
    return chip, 1 - core, z_hi, x


def chip_before(chip, core, z_hi, x):
    return chip - 1, core, z_hi, x


def last_group(chip, core, z_hi, x):
    return (chip, 0, z_hi, x) if core == 1 else (chip - 1, 1, z_hi, x)


def after(block, *earlier):
    return lax.optimization_barrier((block,) + earlier)[0]


VMEM = pl.BlockSpec(memory_space=pltpu.VMEM)
ANY = pl.BlockSpec(memory_space=pl.ANY)


def params(mebibytes):
    return pltpu.CompilerParams(vmem_limit_bytes=mebibytes * 1024 * 1024)


def cost(flops, reads):
    return pl.CostEstimate(flops=flops, bytes_accessed=reads, transcendentals=0)


def copy_all(copies):
    for copy in copies:
        copy.start()
    for copy in copies:
        copy.wait()


def project_kernel(pieces, own, first, other, far, weight, queries, pairs, rows, held, sems):
    n = own.shape[0]
    depth, head_width = weight.shape[1:]
    piece = depth // pieces
    loads = []
    for i, part in enumerate((1, 2, 0)):
        for k in range(pieces):
            source = weight.at[part, pl.ds(k * piece, piece), :]
            at = i * pieces + k
            loads.append(pltpu.make_async_copy(source, held.at[at], sems.at[at]))
    for load in loads:
        load.start()
    for slot, ref in enumerate((own, first, other, far)):
        rows[slot * n : (slot + 1) * n, :] = ref[...]
    for i in range(3):
        total = jnp.zeros((4 * n, head_width), jnp.float32)
        for k in range(pieces):
            at = i * pieces + k
            loads[at].wait()
            total = total + jnp.dot(
                rows[:, k * piece : (k + 1) * piece], held[at], preferred_element_type=jnp.float32
            )
        if i < 2:
            pairs[:, i * head_width : (i + 1) * head_width] = total.astype(jnp.bfloat16)
        else:
            queries[...] = total.astype(jnp.bfloat16)


def project(slots, weight):
    n, width = slots[0].shape
    head_width = weight.shape[2]
    m = 4 * n
    pieces = 2
    return pl.pallas_call(
        functools.partial(project_kernel, pieces),
        in_specs=[VMEM] * 4 + [ANY],
        out_specs=[VMEM] * 2,
        out_shape=[
            jax.ShapeDtypeStruct((m, head_width), jnp.bfloat16),
            jax.ShapeDtypeStruct((m, 2 * head_width), jnp.bfloat16),
        ],
        scratch_shapes=[
            pltpu.VMEM((m, width), jnp.bfloat16),
            pltpu.VMEM((3 * pieces, width // pieces, head_width), jnp.bfloat16),
            pltpu.SemaphoreType.DMA((3 * pieces,)),
        ],
        compiler_params=params(48),
        cost_estimate=cost(2 * m * width * 3 * head_width, 2 * 3 * width * head_width),
    )(*slots, weight)


def attend_kernel(n_queries, n_pairs, start, end, skip, *refs):
    queries = refs[:n_queries]
    pairs = refs[n_queries : n_queries + n_pairs]
    refs = refs[n_queries + n_pairs :]
    if not start:
        top_in, total_in, mixed_in = refs[:3]
        refs = refs[3:]
    if end:
        out = refs[0]
        refs = refs[1:]
    else:
        top_out, total_out, mixed_out = refs[:3]
        refs = refs[3:]
    q_all, kv_all, sems = refs
    head_width = q_all.shape[1]
    heads = head_width // HEAD_DIM
    copies = []
    at = 0
    for i, ref in enumerate(pairs):
        copies.append(pltpu.make_async_copy(ref, kv_all.at[pl.ds(at, ref.shape[0]), :], sems.at[i]))
        at += ref.shape[0]
    for copy in copies:
        copy.start()
    at = 0
    for ref in queries:
        q_all[at : at + ref.shape[0], :] = ref[...]
        at += ref.shape[0]
    for copy in copies:
        copy.wait()
    keys = kv_all.shape[0]

    @pl.loop(0, q_all.shape[0] // TILE)
    def _(i):
        here = pl.ds(pl.multiple_of(i * TILE, TILE), TILE)
        there = pl.ds(pl.multiple_of(skip + i * TILE, TILE), TILE)

        def score(head):
            columns = slice(head * HEAD_DIM, (head + 1) * HEAD_DIM)
            return [
                lax.dot_general(
                    q_all[here, columns],
                    kv_all[k : k + STEP, columns],
                    (((1,), (1,)), ((), ())),
                    preferred_element_type=jnp.float32,
                )
                for k in range(0, keys, STEP)
            ]

        scores = score(0)
        for head in range(heads):
            later = score(head + 1) if head + 1 < heads else None
            columns = slice(head * HEAD_DIM, (head + 1) * HEAD_DIM)
            values = slice(head_width + head * HEAD_DIM, head_width + (head + 1) * HEAD_DIM)
            top = functools.reduce(jnp.maximum, [jnp.max(s, axis=1, keepdims=True) for s in scores])
            if start:
                total = jnp.zeros((TILE, 1), jnp.float32)
                mixed = jnp.zeros((TILE, HEAD_DIM), jnp.float32)
            else:
                before = top_in[there, head * HEAD_DIM : head * HEAD_DIM + 1]
                top = jnp.maximum(top, before)
                factor = jnp.exp2((before - top) * EXP2_SCALE)
                total = total_in[there, head * HEAD_DIM : head * HEAD_DIM + 1] * factor
                mixed = mixed_in[there, columns] * factor
            for j, s in enumerate(scores):
                weights = jnp.exp2((s - top) * EXP2_SCALE)
                total = total + jnp.sum(weights, axis=1, keepdims=True)
                mixed = mixed + jnp.dot(
                    weights.astype(jnp.bfloat16),
                    kv_all[j * STEP : (j + 1) * STEP, values],
                    preferred_element_type=jnp.float32,
                )
            if end:
                out[here, columns] = (mixed / total).astype(jnp.bfloat16)
            else:
                top_out[here, columns] = jnp.broadcast_to(top, (TILE, HEAD_DIM))
                total_out[here, columns] = jnp.broadcast_to(total, (TILE, HEAD_DIM))
                mixed_out[here, columns] = mixed
            scores = later


def attend(queries, pairs, state=(), end=False, skip=0):
    head_width = queries[0].shape[1]
    m = sum(q.shape[0] for q in queries)
    keys = sum(p.shape[0] for p in pairs)
    whole = jax.ShapeDtypeStruct((m, head_width), jnp.float32)
    out_shape = jax.ShapeDtypeStruct((m, head_width), jnp.bfloat16) if end else [whole] * 3
    return pl.pallas_call(
        functools.partial(attend_kernel, len(queries), len(pairs), not state, end, skip),
        in_specs=[VMEM] * len(queries) + [ANY] * len(pairs) + [VMEM] * len(state),
        out_specs=VMEM if end else [VMEM] * 3,
        out_shape=out_shape,
        scratch_shapes=[
            pltpu.VMEM((m, head_width), jnp.bfloat16),
            pltpu.VMEM((keys, 2 * head_width), jnp.bfloat16),
            pltpu.SemaphoreType.DMA((len(pairs),)),
        ],
        compiler_params=params(20),
        cost_estimate=cost(4 * m * keys * head_width, 4 * keys * head_width),
    )(*queries, *pairs, *state)


def mix_kernel(attended, weight, own, first, other, far):
    n = own.shape[0]
    result = jnp.dot(attended[...], weight[...], preferred_element_type=jnp.float32)
    own[...] = result[:n]
    first[...] = result[n : 2 * n].astype(first.dtype)
    other[...] = result[2 * n : 3 * n].astype(jnp.bfloat16)
    far[...] = result[3 * n :].astype(jnp.bfloat16)


def mix(attended, weight, first_type):
    n = attended.shape[0] // 4
    width = weight.shape[1]
    wide = jax.ShapeDtypeStruct((n, width), jnp.float32)
    narrow = jax.ShapeDtypeStruct((n, width), jnp.bfloat16)
    return pl.pallas_call(
        mix_kernel,
        in_specs=[VMEM] * 2,
        out_specs=[VMEM] * 4,
        out_shape=[wide, jax.ShapeDtypeStruct((n, width), first_type), narrow, narrow],
        compiler_params=params(12),
        cost_estimate=cost(8 * n * attended.shape[1] * width, 2 * attended.shape[1] * width),
    )(attended, weight)


def join_kernel(*refs):
    out = refs[-1]
    n = refs[0].shape[0]
    for part in range(2):
        own, other, first, crossed = refs[4 * part : 4 * part + 4]
        total = own[...] + other[...].astype(jnp.float32) + first[...].astype(jnp.float32)
        out[part * n : (part + 1) * n, :] = (total + crossed[...].astype(jnp.float32)).astype(jnp.bfloat16)


def join(upper, lower):
    n, width = upper[0].shape
    return pl.pallas_call(
        join_kernel,
        in_specs=[VMEM] * 8,
        out_specs=VMEM,
        out_shape=jax.ShapeDtypeStruct((2 * n, width), jnp.bfloat16),
        compiler_params=params(12),
        cost_estimate=cost(8 * n * width, 24 * n * width),
    )(*upper, *lower)


def on_device(tokens, qkv_weight, out_weight):
    rows = tokens.shape[0]
    half = rows // 2
    weight = jnp.transpose(qkv_weight, (1, 0, 2))
    core = lax.axis_index("blk") % CORE

    def pass_last(own_pairs, two_on):
        return send(jnp.where(core == 1, own_pairs, two_on), last_group)

    chunk0, chunk1 = tokens[:half], tokens[half:]
    chunk2 = send(chunk0, across_z)
    first0, other0 = send(chunk0, first_way), send(chunk0, other_way)
    first1, other1 = send(chunk1, first_way), send(chunk1, other_way)
    chunk3 = send(after(chunk1, first0), across_z)
    far0, far1 = send(first0, first_way), send(first1, first_way)
    queries0, pairs0 = project((after(chunk0, chunk2, other1, far1), first0, other0, far0), weight)
    two0 = send(pairs0, chip_before)
    first2, other2 = send(chunk2, first_way), send(chunk2, other_way)
    queries1, pairs1 = project((after(chunk1, pairs0), first1, other1, far1), weight)
    two1 = send(pairs1, chip_before)

    far2 = send(after(first2, pairs1), first_way)
    first3, other3 = send(after(chunk3, pairs1), first_way), send(after(chunk3, pairs1), other_way)
    queries2, pairs2 = project((after(chunk2, chunk3), first2, other2, far2), weight)
    last0 = pass_last(pairs0, two0)
    swapped0 = send(two0, other_core)
    two2 = send(after(pairs2, last0), chip_before)

    far3 = send(after(first3, pairs2), first_way)
    last1 = pass_last(pairs1, two1)
    swapped1 = send(two1, other_core)
    queries3, pairs3 = project((chunk3, first3, other3, far3), weight)
    two3 = send(after(pairs3, last1), chip_before)

    queries = [queries0, queries1, queries2, queries3]
    state = attend(queries, [pairs0, two0, swapped0, last0, pairs1, two1, swapped1, last1])
    last2 = pass_last(pairs2, two2)
    swapped2 = send(two2, other_core)
    two3 = after(two3, state[0], last2)
    last3 = pass_last(pairs3, two3)
    swapped3 = send(two3, other_core)
    pairs = [pairs2, two2, swapped2, last2, pairs3, two3, swapped3, last3]

    m = 4 * half
    theirs = attend(queries[2:], pairs, state, end=True, skip=2 * m)
    ours = attend(queries[:2], pairs, state, end=True)

    def begin(attended, *earlier):
        own, first, other, far = mix(after(attended, *earlier), out_weight, jnp.float32)
        return own, first, send(far, other_way), send(other, first_way)

    def finish(own, first, from_far, from_other, *earlier):
        first = (first + from_far.astype(jnp.float32)).astype(jnp.bfloat16)
        return own + from_other.astype(jnp.float32) + send(after(first, *earlier), other_way).astype(jnp.float32)

    own, first, other, far = mix(theirs[:m], out_weight, jnp.bfloat16)
    arriving = [send(far, half_way), send(first, other_way), send(other, first_way)]
    begun3 = begin(theirs[m:])
    leaving2 = (after(own, ours) + sum(part.astype(jnp.float32) for part in arriving)).astype(jnp.bfloat16)
    crossed2 = send(leaving2, across_z)
    begun0 = begin(ours[:m], begun3[2], begun3[3], leaving2)
    leaving3 = finish(*begun3, leaving2).astype(jnp.bfloat16)
    crossed3 = send(leaving3, across_z)
    begun1 = begin(ours[m:], leaving3)
    def last_terms(own, first, from_far, from_other):
        first = (first + from_far.astype(jnp.float32)).astype(jnp.bfloat16)
        return own, from_other, send(first, other_way)

    return join(last_terms(*begun0) + (crossed2,), last_terms(*begun1) + (crossed3,))


def solution(mesh):
    in_specs = (P(("blk", "uly"), None), P(None, None, "uly"), P("uly", None))
    out_specs = P(("blk", "uly"), None)
    return jax.shard_map(
        on_device, mesh=mesh, in_specs=in_specs, out_specs=out_specs, check_vma=False
    )
```
